128 devices in a mesh: dp: 4 (over x), expert: 32 (over y, z, core).
Axes of the slice: x: 4, y: 4, z: 4, core: 2. Of those that a mesh axis runs over, the one named last changes fastest.
Arguments:
- hidden_states: bfloat16 [8192, 3584], P(('dp', 'expert')), may hold values from -6 to 6
- router_scores: float32 [8192, 8], P(('dp', 'expert')), may hold values from 0.05 to 1
- copy_route: int32 [8192, 8], P(('dp', 'expert')), may hold values from 0 to 63, all different within a row; in each aligned block of 64 rows (0 to 63, 64 to 127, ...) at most 12 rows name the same one
- slot_source: int32 [32], replicated, may hold values from 0 to 31, as said below
- gate_proj: bfloat16 [32, 3584, 2048], P('expert', None, 'dp'), may hold values from -0.09375 to 0.09375
- up_proj: bfloat16 [32, 3584, 2048], P('expert', None, 'dp'), may hold values from -0.09375 to 0.09375
- down_proj: bfloat16 [32, 2048, 3584], P('expert', 'dp'), may hold values from -0.125 to 0.125
Outputs:
- moe_output: bfloat16 [8192, 3584], P(('dp', 'expert'))
The draws below stay inside these ranges and needn't reach their ends.
Inputs may be any that keep to these rules, and one draw needn't show every extreme that they name: `copy_route`: copies 0 to 31 are the native experts; copy 32 + s is redundant slot s, held on index s of expert. A token's 8 routes name different copies. Within the 64 rows of one device, no copy is named by more than 12 routes. `slot_source`: 8 distinct experts appear, each in exactly 4 slots.
All inputs are finite; a program needn't handle non-finite values.
Results may differ from the reference program's by a relative error of at most 0.017.
Values may be sent and summed in bfloat16 or wider, within the bound.
No kernel may reach another device: no remote copies, remote signals or barrier semaphores. Data moves between devices by JAX's collectives and lax.ppermute only.
A program may use at most 192 MiB of HBM per device.

```python
import math
import jax
import jax.numpy as jnp
import numpy as np
from jax import lax

D = 3584
HID = 2048
TOP = 8
TOK_DEV = 64
EXPERTS = 32
CAP = 12
TOKENS = 8192
N_DP = 4


def draw_slot_source(key, part):
    key = jax.random.fold_in(key, 11)
    middle = 1 + jax.random.permutation(jax.random.fold_in(key, 1), EXPERTS - 2)
    hot_set = jnp.concatenate((jnp.array([0, EXPERTS - 1], jnp.int32), middle[:EXPERTS // 4 - 2].astype(jnp.int32)))
    slot_order = jax.random.permutation(jax.random.fold_in(key, 2), EXPERTS)
    return hot_set[slot_order % (EXPERTS // 4)].astype(jnp.int32)


def shard_levels(own_key, extent, split, least, largest):
    factor_of, own = 1.0, jax.random.fold_in(own_key, 6)
    for position, parts in split:
        steps = jnp.exp(jax.random.uniform(jax.random.fold_in(own, position), (parts,), jnp.float32, least / len(split), largest / len(split)))
        factor_of = factor_of * jnp.repeat(steps, extent[position] // parts).reshape([-1 if axis == position else 1 for axis in range(len(extent))])
    return factor_of


def routed_block(own_key, own, number, rows, amount, top, reach, slope):
    order = jax.random.permutation(own_key, amount)
    packed, common = shares(amount, rows * top, reach, slope, True), shares(amount, rows * top, reach, slope, False)
    places = jnp.arange(amount)

    def named(tallies, turn):
        used = int((tallies > 0).sum())
        fixed = max(1, used // 4)
        passed = fixed + (places - fixed + turn * (used - fixed)) % max(1, amount - fixed)
        return jnp.zeros((amount,), jnp.int32).at[order[jnp.where(places < fixed, places, passed)]].set(jnp.asarray(tallies, jnp.int32))

    tallies = jnp.where(number % 4 == 0, named(packed, number // 4), named(common, number - number // 4 - 1))
    mixed = jax.random.permutation(jax.random.fold_in(own, 3), amount)
    giver, sink = mixed[0:amount // 2 * 2:2], mixed[1:amount // 2 * 2:2]
    margin = jnp.minimum(tallies[giver] - 1, reach - tallies[sink]) // 2
    margin = jnp.where((giver == order[0]) | (sink == order[0]) | (tallies[sink] == 0), 0, jnp.maximum(margin, 0))
    passed = jax.random.randint(jax.random.fold_in(own, 4), (amount // 2,), 0, 1 << 20) % (margin + 1)
    tallies = tallies.at[giver].add(-passed).at[sink].add(passed)
    labels = jnp.searchsorted(jnp.cumsum(tallies), jnp.arange(rows * top), side="right").astype(jnp.int32)
    listing = labels.reshape(top, rows).T
    listing = listing[jax.random.permutation(jax.random.fold_in(own, 1), rows)]
    turn = jax.random.randint(jax.random.fold_in(own, 2), (rows, 1), 0, top)
    return jnp.take_along_axis(listing, (jnp.arange(top)[None, :] + turn) % top, axis=1)


def shares(amount, total, bound, skew, full):
    portions = [(1 << 20) // math.isqrt(standing ** skew) + 1 for standing in range(1, amount + 1)]
    largest = bound if full else min(bound, max(-(-total // amount), total * portions[0] // sum(portions)))
    least = 1 if total - largest >= amount - 1 else 0
    given, surplus = [largest] + [least] * (amount - 1), total - largest - least * (amount - 1)
    while surplus > 0:
        candidates = [i for i in range(1, amount) if given[i] < largest] or [i for i in range(1, amount) if given[i] < bound]
        mass, remaining = sum([portions[i] for i in candidates]), surplus
        for i in candidates:
            addition = min(bound - given[i], max(1, remaining * portions[i] // mass), surplus)
            given[i] = given[i] + addition
            surplus = surplus - addition
    return np.array(given)


def noise(key, dims, width, limit, cuts=(), kind=jnp.bfloat16):
    gain = shard_levels(key, dims, cuts, -0.22, 0.18) if cuts else 1.0
    values = jax.random.normal(key, dims, jnp.float32) * width * gain
    return jnp.minimum(jnp.maximum(values, -limit), limit).astype(kind)


def setup_inputs(seed: int = 0) -> dict:
    splits = jax.random.split(jax.random.key(seed), 8)
    hidden_states = noise(splits[0], (TOKENS, D), 1.0, 6.0, ((0, 128),))
    router_scores = jnp.clip(jnp.exp(math.log(1.0) - 2.9957323 * jax.random.uniform(splits[1], (TOKENS, TOP), jnp.float32) ** shard_levels(splits[1], (TOKENS, TOP), ((0, 128),), -0.2, 0.2)), 0.05, 1.0)
    copy_route_keys = jax.random.split(jax.random.fold_in(splits[2], 1), TOKENS // TOK_DEV)
    copy_route_turns = jax.random.permutation(jax.random.fold_in(splits[2], 3), TOKENS // TOK_DEV)
    copy_route = jax.vmap(lambda own, number: routed_block(jax.random.fold_in(splits[2], 2), own, number, TOK_DEV, 2 * EXPERTS, TOP, CAP, 2))(copy_route_keys, copy_route_turns).reshape((TOKENS, TOP))
    slot_source = draw_slot_source(jax.random.fold_in(splits[7], 71), 0)
    gate_proj = noise(splits[4], (EXPERTS, D, HID), D ** -0.5, 0.09375, ((0, 32), (2, 4)))
    up_proj = noise(splits[5], (EXPERTS, D, HID), D ** -0.5, 0.09375, ((0, 32), (2, 4)))
    down_proj = noise(splits[6], (EXPERTS, HID, D), HID ** -0.5, 0.125, ((0, 32), (1, 4)))
    return dict(hidden_states=hidden_states, router_scores=router_scores, copy_route=copy_route, slot_source=slot_source, gate_proj=gate_proj, up_proj=up_proj, down_proj=down_proj)


route_scale = 2.5


def reference(hidden_states, router_scores, copy_route, slot_source, gate_proj, up_proj, down_proj):
    gate_weights = route_scale * router_scores / jnp.sum(router_scores, axis=1, keepdims=True)
    slot_index = jnp.clip(copy_route - EXPERTS, 0, EXPERTS - 1).astype(jnp.int32)
    expert_ids = jnp.where(copy_route < EXPERTS, copy_route, slot_source[slot_index]).astype(jnp.int32)
    quarter = HID // N_DP

    def one_expert(running, expert_index):
        chosen = jnp.sum(jnp.where(expert_ids == expert_index, gate_weights, jnp.zeros_like(gate_weights)), axis=1)
        gate_value = jnp.dot(hidden_states, gate_proj[expert_index], preferred_element_type=jnp.float32)
        up_value = jnp.dot(hidden_states, up_proj[expert_index], preferred_element_type=jnp.float32)
        activated = (jax.nn.silu(gate_value) * up_value).astype(jnp.bfloat16)
        accumulated = jnp.zeros((TOKENS, D), jnp.float32)
        for quarter_index in range(N_DP):
            lower = quarter_index * quarter
            partial_sum = jnp.dot(activated[:, lower:lower + quarter], down_proj[expert_index, lower:lower + quarter], preferred_element_type=jnp.float32).astype(jnp.bfloat16)
            partial_sum = lax.optimization_barrier(partial_sum)
            accumulated = accumulated + partial_sum.astype(jnp.float32)
        expert_out = lax.optimization_barrier(accumulated.astype(jnp.bfloat16))
        return running + chosen[:, None] * expert_out.astype(jnp.float32), None

    running, unused = lax.scan(one_expert, jnp.zeros((TOKENS, D), jnp.float32), jnp.arange(EXPERTS, dtype=jnp.int32))
    return running.astype(jnp.bfloat16)
```

```python
import functools

import jax
import jax.numpy as jnp
from jax import lax
from jax.experimental import pallas as pl
from jax.experimental.pallas import tpu as pltpu
from jax.sharding import Mesh
from jax.sharding import PartitionSpec as P

ROUTE_SCALE = 2.5
AXES = ("x", "y", "z", "core")
PAD = 128
CHUNK = 16
GROUP = 2
COLS = 512


def token_gates(scores, route, source, experts):
    gates = ROUTE_SCALE * scores / jnp.sum(scores, axis=1, keepdims=True)
    native = jnp.arange(experts, dtype=jnp.int32)
    copies = jnp.arange(2 * experts, dtype=jnp.int32)
    held = jnp.concatenate((native, source))
    routed = route[:, :, None] == copies
    ids = jnp.sum(jnp.where(routed, held, 0), axis=2)
    return jnp.sum(jnp.where(ids[:, :, None] == native, gates[:, :, None], 0.0), axis=1)


def ffn_kernel(experts, ids, x_ref, ga, gb, ua, ub, da, db, o_ref, gate, up, down, act, sems):
    width, hid = ga.shape
    rows = x_ref.shape[0] * x_ref.shape[1] * x_ref.shape[2]
    copies = (
        pltpu.make_async_copy(ga, gate.at[0], sems.at[0]),
        pltpu.make_async_copy(ua, up.at[0], sems.at[1]),
        pltpu.make_async_copy(gb, gate.at[1], sems.at[2]),
        pltpu.make_async_copy(ub, up.at[1], sems.at[3]),
        pltpu.make_async_copy(da, down.at[pl.ds(0, hid)], sems.at[4]),
        pltpu.make_async_copy(db, down.at[pl.ds(hid, hid)], sems.at[5]),
    )
    first = pl.program_id(0) == 0

    @pl.when(first)
    def _():
        for copy in copies:
            copy.start()

    def ready(number):
        @pl.when(first)
        def _():
            copies[number].wait()

    block = x_ref[...].reshape(rows, width + PAD)
    tokens = block[:, :width]
    shares = block[:, width:].astype(jnp.float32)
    lane = lax.broadcasted_iota(jnp.int32, shares.shape, 1)
    for k in range(2):
        mine = (lane == ids[k]) | (lane == ids[k] + experts)
        share = jnp.sum(jnp.where(mine, shares, 0.0), axis=1, keepdims=True)
        ready(2 * k)
        g = jnp.dot(tokens, gate[k], preferred_element_type=jnp.float32)
        ready(2 * k + 1)
        u = jnp.dot(tokens, up[k], preferred_element_type=jnp.float32)
        act[:, k * hid : (k + 1) * hid] = (g / (1.0 + jnp.exp(-g)) * u * share).astype(act.dtype)
    ready(4)
    ready(5)
    for c in range(0, width, COLS):
        part = jnp.dot(act[...], down[:, c : c + COLS], preferred_element_type=jnp.float32)
        part = part.astype(o_ref.dtype).reshape(x_ref.shape[:3] + (COLS,))
        for j in range(x_ref.shape[0]):
            o_ref[:, j, :, c : c + COLS] = part[j]


def ffn(ids, rows, weights, planes, spots, chunk, experts):
    width, hid = weights[0].shape
    amount = planes * spots * chunk
    group = GROUP
    tile = group * spots * chunk
    return pl.pallas_call(
        functools.partial(ffn_kernel, experts),
        grid_spec=pltpu.PrefetchScalarGridSpec(
            num_scalar_prefetch=1,
            grid=(planes // group,),
            in_specs=[
                pl.BlockSpec((group, spots, chunk, width + PAD), lambda i, s: (i, 0, 0, 0))
            ]
            + [pl.BlockSpec(memory_space=pl.ANY)] * 6,
            out_specs=pl.BlockSpec((spots, group, chunk, width), lambda i, s: (0, i, 0, 0)),
            scratch_shapes=[
                pltpu.VMEM((2, width, hid), jnp.bfloat16),
                pltpu.VMEM((2, width, hid), jnp.bfloat16),
                pltpu.VMEM((2 * hid, width), jnp.bfloat16),
                pltpu.VMEM((tile, 2 * hid), jnp.bfloat16),
                pltpu.SemaphoreType.DMA((6,)),
            ],
        ),
        out_shape=jax.ShapeDtypeStruct((spots, planes, chunk, width), jnp.bfloat16),
        compiler_params=pltpu.CompilerParams(vmem_limit_bytes=56 * 1024 * 1024),
        cost_estimate=pl.CostEstimate(
            flops=amount * width * hid * 12,
            bytes_accessed=amount * width * 4 + 12 * width * hid,
            transcendentals=amount * hid * 2,
        ),
    )(ids, rows.reshape(planes, spots, chunk, width + PAD), *weights)


def per_device(hidden, scores, route, source, gate_proj, up_proj, down_proj):
    planes, spots = lax.axis_size("x"), lax.axis_size("y") * lax.axis_size("z")
    experts = 2 * spots
    tokens, width = hidden.shape
    swap = [(0, 1), (1, 0)]
    dense = token_gates(scores, route, source, experts)
    high = lax.reduce_precision(dense, 8, 7)
    low = dense - high
    filler = jnp.zeros((tokens, PAD - 2 * experts), jnp.bfloat16)
    packed = jnp.concatenate(
        (hidden, high.astype(jnp.bfloat16), low.astype(jnp.bfloat16), filler), axis=1
    )
    weights = []
    for own in (gate_proj[0], up_proj[0], down_proj[0]):
        weights += [own, lax.ppermute(own, "core", swap)]
    core = lax.axis_index("core")
    pair = (lax.axis_index("y") * lax.axis_size("z") + lax.axis_index("z")) * 2
    ids = jnp.stack((pair + core, pair + 1 - core)).astype(jnp.int32)
    results = []
    for start in range(0, tokens, CHUNK):
        rows = lax.all_gather(packed[start : start + CHUNK], ("x", "y", "z"), tiled=True)
        part = ffn(ids, rows, weights, planes, spots, CHUNK, experts)
        part = part.reshape(-1, width)
        part = lax.psum_scatter(part, ("y", "z"), scatter_dimension=0, tiled=True)
        results.append(lax.psum_scatter(part, "x", scatter_dimension=0, tiled=True))
    return jnp.concatenate(results, axis=0)


def solution(mesh):
    planes, experts = mesh.shape["dp"], mesh.shape["expert"]
    side = int(round((experts // 2) ** 0.5))
    grid = Mesh(mesh.devices.reshape(planes, side, side, 2), AXES)
    rows, spread = P(AXES, None), ("y", "z", "core")
    placed = (
        rows,
        rows,
        rows,
        P(),
        P(spread, None, "x"),
        P(spread, None, "x"),
        P(spread, "x", None),
    )
    return jax.shard_map(
        per_device, mesh=grid, in_specs=placed, out_specs=rows, check_vma=False
    )
```

```python
import functools

import jax
import jax.numpy as jnp
from jax import lax
from jax.experimental import pallas as pl
from jax.experimental.pallas import tpu as pltpu
from jax.sharding import Mesh
from jax.sharding import PartitionSpec as P

ROUTE_SCALE = 2.5
AXES = ("x", "y", "z", "core")
ORDERS = (("x", "y", "z"), ("y", "z", "x"), ("z", "x", "y"))
PAD = 128
COUNTS = (24, 24, 16)
COLS = 512


def token_gates(scores, route, source, experts):
    gates = ROUTE_SCALE * scores / jnp.sum(scores, axis=1, keepdims=True)
    native = jnp.arange(experts, dtype=jnp.int32)
    copies = jnp.arange(2 * experts, dtype=jnp.int32)
    held = jnp.concatenate((native, source))
    routed = route[:, :, None] == copies
    ids = jnp.sum(jnp.where(routed, held, 0), axis=2)
    return jnp.sum(jnp.where(ids[:, :, None] == native, gates[:, :, None], 0.0), axis=1)


def ffn_kernel(experts, counts, ids, *refs):
    n = len(counts)
    pieces, weights, outs = refs[:n], refs[n : n + 6], refs[n + 6 : 2 * n + 6]
    x, gate, up, down, act, o, x_sems, w_sems, o_sems = refs[2 * n + 6 :]
    ga, gb, ua, ub, da, db = weights
    width, hid = ga.shape
    starts = [sum(counts[:j]) for j in range(n)]
    arrive = [
        pltpu.make_async_copy(pieces[j], x.at[pl.ds(starts[j], counts[j])], x_sems.at[j])
        for j in range(n)
    ]
    load = [
        pltpu.make_async_copy(ga, gate.at[0], w_sems.at[0]),
        pltpu.make_async_copy(ua, up.at[0], w_sems.at[1]),
        pltpu.make_async_copy(gb, gate.at[1], w_sems.at[2]),
        pltpu.make_async_copy(ub, up.at[1], w_sems.at[3]),
        pltpu.make_async_copy(da, down.at[pl.ds(0, hid)], w_sems.at[4]),
        pltpu.make_async_copy(db, down.at[pl.ds(hid, hid)], w_sems.at[5]),
    ]
    load[0].start()
    for copy in arrive[:2]:
        copy.start()
    load[0].wait()
    gates = []
    for j in range(n):
        arrive[j].wait()
        if j == 0:
            for copy in arrive[2:]:
                copy.start()
            load[1].start()
        rows = x[starts[j] : starts[j] + counts[j], :width]
        gates.append(jnp.dot(rows, gate[0], preferred_element_type=jnp.float32))
    for k in range(2):
        if k == 0:
            g = jnp.concatenate(gates)
        else:
            load[2].wait()
            load[4].start()
            load[5].start()
            g = jnp.dot(x[:, :width], gate[k], preferred_element_type=jnp.float32)
        load[2 * k + 1].wait()
        if k == 0:
            load[2].start()
            load[3].start()
        u = jnp.dot(x[:, :width], up[k], preferred_element_type=jnp.float32)
        shares = x[:, width:].astype(jnp.float32)
        lane = lax.broadcasted_iota(jnp.int32, shares.shape, 1)
        mine = (lane == ids[k]) | (lane == ids[k] + experts)
        share = jnp.sum(jnp.where(mine, shares, 0.0), axis=1, keepdims=True)
        act[:, k * hid : (k + 1) * hid] = (g / (1.0 + jnp.exp(-g)) * u * share).astype(act.dtype)
    load[4].wait()
    load[5].wait()
    leave = []
    for i, c in enumerate(range(0, width, COLS)):
        part = jnp.dot(act[...], down[:, c : c + COLS], preferred_element_type=jnp.float32)
        o[:, c : c + COLS] = part.astype(o.dtype)
        for j in range(n):
            copy = pltpu.make_async_copy(
                o.at[pl.ds(starts[j], counts[j]), pl.ds(c, COLS)],
                outs[j].at[:, pl.ds(c, COLS)],
                o_sems.at[i, j],
            )
            copy.start()
            leave.append(copy)
    for copy in leave:
        copy.wait()


def ffn(ids, pieces, weights, experts):
    width, hid = weights[0].shape
    counts = tuple(piece.shape[0] for piece in pieces)
    amount, n = sum(counts), len(counts)
    anywhere = pl.BlockSpec(memory_space=pl.ANY)
    return pl.pallas_call(
        functools.partial(ffn_kernel, experts, counts),
        in_specs=[pl.BlockSpec(memory_space=pltpu.SMEM)] + [anywhere] * (n + 6),
        out_specs=[anywhere] * n,
        scratch_shapes=[
            pltpu.VMEM((amount, width + PAD), jnp.bfloat16),
            pltpu.VMEM((2, width, hid), jnp.bfloat16),
            pltpu.VMEM((2, width, hid), jnp.bfloat16),
            pltpu.VMEM((2 * hid, width), jnp.bfloat16),
            pltpu.VMEM((amount, 2 * hid), jnp.bfloat16),
            pltpu.VMEM((amount, width), jnp.bfloat16),
            pltpu.SemaphoreType.DMA((n,)),
            pltpu.SemaphoreType.DMA((6,)),
            pltpu.SemaphoreType.DMA((width // COLS, n)),
        ],
        out_shape=[jax.ShapeDtypeStruct((count, width), jnp.bfloat16) for count in counts],
        compiler_params=pltpu.CompilerParams(vmem_limit_bytes=50 * 1024 * 1024),
        cost_estimate=pl.CostEstimate(
            flops=amount * width * hid * 12,
            bytes_accessed=amount * width * 4 + 12 * width * hid,
            transcendentals=amount * hid * 2,
        ),
    )(ids, *pieces, *weights)


def ring(axis, size, way):
    pairs = []
    for i in range(size):
        pairs += [(2 * i, (i + way) % size * 2), (2 * i + 1, (i - way) % size * 2 + 1)]
    return lambda block: lax.ppermute(block, (axis, "core"), pairs)


def meet(axis, size, first):
    pairs = []
    for i in range(size):
        for core in range(2):
            j = i ^ 1 if (core == 0) == first else size - 1 - i
            pairs.append((2 * i + core, 2 * j + core))
    return lambda block: lax.ppermute(block, (axis, "core"), pairs)


def double(block, axis):
    for first in (True, False):
        block = jnp.concatenate((block, meet(axis, lax.axis_size(axis), first)(block)), axis=0)
    return block


def add(one, other):
    return (one.astype(jnp.float32) + other.astype(jnp.float32)).astype(one.dtype)


def halve(totals, axes):
    for first in (False, True):
        halves = [jnp.split(total, 2) for total in totals]
        arrived = lax.optimization_barrier(
            [meet(a, lax.axis_size(a), first)(sent) for a, (_, sent) in zip(axes, halves)]
        )
        totals = [add(kept, other) for (kept, _), other in zip(halves, arrived)]
    return totals


def per_device(hidden, scores, route, source, gate_proj, up_proj, down_proj):
    spots = lax.axis_size("y") * lax.axis_size("z")
    experts = 2 * spots
    tokens, width = hidden.shape
    swap = [(0, 1), (1, 0)]
    dense = token_gates(scores, route, source, experts)
    high = lax.reduce_precision(dense, 8, 7)
    low = dense - high
    filler = jnp.zeros((tokens, PAD - 2 * experts), jnp.bfloat16)
    packed = jnp.concatenate(
        (hidden, high.astype(jnp.bfloat16), low.astype(jnp.bfloat16), filler), axis=1
    )
    weights = []
    for own in (gate_proj[0], up_proj[0], down_proj[0]):
        weights += [own, lax.ppermute(own, "core", swap)]
    core = lax.axis_index("core")
    pair = (lax.axis_index("y") * lax.axis_size("z") + lax.axis_index("z")) * 2
    ids = jnp.stack((pair + core, pair + 1 - core)).astype(jnp.int32)

    blocks, start = [], 0
    for count in COUNTS:
        blocks.append(packed[start : start + count])
        start += count
    for phase in range(2):
        blocks = [double(block, order[phase]) for block, order in zip(blocks, ORDERS)]
        if phase == 0:
            blocks = lax.optimization_barrier(blocks)
        else:
            blocks, weights = lax.optimization_barrier((blocks, weights))
    sends = [ring(order[2], lax.axis_size(order[2]), 1) for order in ORDERS]
    steps, done = [blocks], []
    for step in range(lax.axis_size("x") - 1):
        arriving = [send(block) for send, block in zip(sends, steps[-1])]
        done.append(ffn(ids, steps[-1], weights, experts))
        arriving, done[-1] = lax.optimization_barrier((arriving, done[-1]))
        steps.append(arriving)
    done.append(ffn(ids, steps[-1], weights, experts))
    totals = list(done[-1])
    backs = [ring(order[2], lax.axis_size(order[2]), -1) for order in ORDERS]
    for pieces in done[-2::-1]:
        arrived = lax.optimization_barrier([back(t) for back, t in zip(backs, totals)])
        totals = [add(*pair) for pair in zip(arrived, pieces)]
    for phase in (1, 0):
        totals = halve(totals, [order[phase] for order in ORDERS])
    return jnp.concatenate(totals, axis=0)


def solution(mesh):
    planes, experts = mesh.shape["dp"], mesh.shape["expert"]
    side = int(round((experts // 2) ** 0.5))
    grid = Mesh(mesh.devices.reshape(planes, side, side, 2), AXES)
    rows, held = P(AXES, None), ("y", "z", "core")
    placed = (
        rows,
        rows,
        rows,
        P(),
        P(held, None, "x"),
        P(held, None, "x"),
        P(held, "x", None),
    )
    return jax.shard_map(
        per_device, mesh=grid, in_specs=placed, out_specs=rows, check_vma=False
    )
```

```python
import functools

import jax
import jax.numpy as jnp
from jax import lax
from jax.experimental import pallas as pl
from jax.experimental.pallas import tpu as pltpu
from jax.sharding import Mesh
from jax.sharding import PartitionSpec as P

ROUTE_SCALE = 2.5
AXES = ("x", "y", "z", "core")
ORDERS = (("x", "y", "z"), ("y", "z", "x"), ("z", "x", "y"))
PAD = 128
COUNTS = (22, 21, 21)
COLS = 512


def token_gates(scores, route, source, experts):
    gates = ROUTE_SCALE * scores / jnp.sum(scores, axis=1, keepdims=True)
    native = jnp.arange(experts, dtype=jnp.int32)
    copies = jnp.arange(2 * experts, dtype=jnp.int32)
    held = jnp.concatenate((native, source))
    routed = route[:, :, None] == copies
    ids = jnp.sum(jnp.where(routed, held, 0), axis=2)
    return jnp.sum(jnp.where(ids[:, :, None] == native, gates[:, :, None], 0.0), axis=1)


def ffn_kernel(experts, counts, ids, *refs):
    n = len(counts)
    pieces, weights, outs = refs[:n], refs[n : n + 6], refs[n + 6 : 2 * n + 6]
    x, gate, up, down, act, o, x_sems, w_sems, o_sems = refs[2 * n + 6 :]
    ga, gb, ua, ub, da, db = weights
    width, hid = ga.shape
    starts = [sum(counts[:j]) for j in range(n)]
    arrive = [
        pltpu.make_async_copy(pieces[j], x.at[pl.ds(starts[j], counts[j])], x_sems.at[j])
        for j in range(n)
    ]
    load = [
        pltpu.make_async_copy(ga, gate.at[0], w_sems.at[0]),
        pltpu.make_async_copy(ua, up.at[0], w_sems.at[1]),
        pltpu.make_async_copy(gb, gate.at[1], w_sems.at[2]),
        pltpu.make_async_copy(ub, up.at[1], w_sems.at[3]),
        pltpu.make_async_copy(da, down.at[pl.ds(0, hid)], w_sems.at[4]),
        pltpu.make_async_copy(db, down.at[pl.ds(hid, hid)], w_sems.at[5]),
    ]
    load[0].start()
    for copy in arrive[:2]:
        copy.start()
    load[0].wait()
    gates = []
    for j in range(n):
        arrive[j].wait()
        if j == 0:
            for copy in arrive[2:]:
                copy.start()
            load[1].start()
        rows = x[starts[j] : starts[j] + counts[j], :width]
        gates.append(jnp.dot(rows, gate[0], preferred_element_type=jnp.float32))
    for k in range(2):
        if k == 0:
            g = jnp.concatenate(gates)
        else:
            load[2].wait()
            load[4].start()
            load[5].start()
            g = jnp.dot(x[:, :width], gate[k], preferred_element_type=jnp.float32)
        load[2 * k + 1].wait()
        if k == 0:
            load[2].start()
            load[3].start()
        u = jnp.dot(x[:, :width], up[k], preferred_element_type=jnp.float32)
        shares = x[:, width:].astype(jnp.float32)
        lane = lax.broadcasted_iota(jnp.int32, shares.shape, 1)
        mine = (lane == ids[k]) | (lane == ids[k] + experts)
        share = jnp.sum(jnp.where(mine, shares, 0.0), axis=1, keepdims=True)
        act[:, k * hid : (k + 1) * hid] = (g / (1.0 + jnp.exp(-g)) * u * share).astype(act.dtype)
    load[4].wait()
    load[5].wait()
    leave = []
    for i, c in enumerate(range(0, width, COLS)):
        part = jnp.dot(act[...], down[:, c : c + COLS], preferred_element_type=jnp.float32)
        o[:, c : c + COLS] = part.astype(o.dtype)
        for j in range(n):
            copy = pltpu.make_async_copy(
                o.at[pl.ds(starts[j], counts[j]), pl.ds(c, COLS)],
                outs[j].at[:, pl.ds(c, COLS)],
                o_sems.at[i, j],
            )
            copy.start()
            leave.append(copy)
    for copy in leave:
        copy.wait()


def ffn(ids, pieces, weights, experts):
    width, hid = weights[0].shape
    counts = tuple(piece.shape[0] for piece in pieces)
    amount, n = sum(counts), len(counts)
    anywhere = pl.BlockSpec(memory_space=pl.ANY)
    return pl.pallas_call(
        functools.partial(ffn_kernel, experts, counts),
        in_specs=[pl.BlockSpec(memory_space=pltpu.SMEM)] + [anywhere] * (n + 6),
        out_specs=[anywhere] * n,
        scratch_shapes=[
            pltpu.VMEM((amount, width + PAD), jnp.bfloat16),
            pltpu.VMEM((2, width, hid), jnp.bfloat16),
            pltpu.VMEM((2, width, hid), jnp.bfloat16),
            pltpu.VMEM((2 * hid, width), jnp.bfloat16),
            pltpu.VMEM((amount, 2 * hid), jnp.bfloat16),
            pltpu.VMEM((amount, width), jnp.bfloat16),
            pltpu.SemaphoreType.DMA((n,)),
            pltpu.SemaphoreType.DMA((6,)),
            pltpu.SemaphoreType.DMA((width // COLS, n)),
        ],
        out_shape=[jax.ShapeDtypeStruct((count, width), jnp.bfloat16) for count in counts],
        compiler_params=pltpu.CompilerParams(vmem_limit_bytes=50 * 1024 * 1024),
        cost_estimate=pl.CostEstimate(
            flops=amount * width * hid * 12,
            bytes_accessed=amount * width * 4 + 12 * width * hid,
            transcendentals=amount * hid * 2,
        ),
    )(ids, *pieces, *weights)


def ring(axis, size, way):
    pairs = []
    for i in range(size):
        pairs += [(2 * i, (i + way) % size * 2), (2 * i + 1, (i - way) % size * 2 + 1)]
    return lambda block: lax.ppermute(block, (axis, "core"), pairs)


def meet(axis, size, first):
    pairs = []
    for i in range(size):
        for core in range(2):
            j = i ^ 1 if (core == 0) == first else size - 1 - i
            pairs.append((2 * i + core, 2 * j + core))
    return lambda block: lax.ppermute(block, (axis, "core"), pairs)


def double(block, axis):
    for first in (True, False):
        block = jnp.concatenate((block, meet(axis, lax.axis_size(axis), first)(block)), axis=0)
    return block


def add(one, other):
    return (one.astype(jnp.float32) + other.astype(jnp.float32)).astype(one.dtype)


def halve(totals, axes):
    for first in (False, True):
        halves = [jnp.split(total, 2) for total in totals]
        arrived = lax.optimization_barrier(
            [meet(a, lax.axis_size(a), first)(sent) for a, (_, sent) in zip(axes, halves)]
        )
        totals = [add(kept, other) for (kept, _), other in zip(halves, arrived)]
    return totals


def per_device(hidden, scores, route, source, gate_proj, up_proj, down_proj):
    spots = lax.axis_size("y") * lax.axis_size("z")
    experts = 2 * spots
    tokens, width = hidden.shape
    swap = [(0, 1), (1, 0)]
    dense = token_gates(scores, route, source, experts)
    high = lax.reduce_precision(dense, 8, 7)
    low = dense - high
    filler = jnp.zeros((tokens, PAD - 2 * experts), jnp.bfloat16)
    packed = jnp.concatenate(
        (hidden, high.astype(jnp.bfloat16), low.astype(jnp.bfloat16), filler), axis=1
    )
    weights = []
    for own in (gate_proj[0], up_proj[0], down_proj[0]):
        weights += [own, lax.ppermute(own, "core", swap)]
    core = lax.axis_index("core")
    pair = (lax.axis_index("y") * lax.axis_size("z") + lax.axis_index("z")) * 2
    ids = jnp.stack((pair + core, pair + 1 - core)).astype(jnp.int32)

    blocks, start = [], 0
    for count in COUNTS:
        blocks.append(packed[start : start + count])
        start += count
    for phase in range(2):
        blocks = [double(block, order[phase]) for block, order in zip(blocks, ORDERS)]
        if phase == 0:
            blocks, weights = lax.optimization_barrier((blocks, weights))
        else:
            blocks = lax.optimization_barrier(blocks)
    sends = [ring(order[2], lax.axis_size(order[2]), 1) for order in ORDERS]
    steps, done = [blocks], []
    for step in range(lax.axis_size("x") - 1):
        arriving = [send(block) for send, block in zip(sends, steps[-1])]
        done.append(ffn(ids, steps[-1], weights, experts))
        arriving, done[-1] = lax.optimization_barrier((arriving, done[-1]))
        steps.append(arriving)
    done.append(ffn(ids, steps[-1], weights, experts))
    totals = list(done[-1])
    backs = [ring(order[2], lax.axis_size(order[2]), -1) for order in ORDERS]
    for pieces in done[-2::-1]:
        arrived = lax.optimization_barrier([back(t) for back, t in zip(backs, totals)])
        totals = [add(*pair) for pair in zip(arrived, pieces)]
    for phase in (1, 0):
        totals = halve(totals, [order[phase] for order in ORDERS])
    return jnp.concatenate(totals, axis=0)


def solution(mesh):
    planes, experts = mesh.shape["dp"], mesh.shape["expert"]
    side = int(round((experts // 2) ** 0.5))
    grid = Mesh(mesh.devices.reshape(planes, side, side, 2), AXES)
    rows, held = P(AXES, None), ("y", "z", "core")
    placed = (
        rows,
        rows,
        rows,
        P(),
        P(held, None, "x"),
        P(held, None, "x"),
        P(held, "x", None),
    )
    return jax.shard_map(
        per_device, mesh=grid, in_specs=placed, out_specs=rows, check_vma=False
    )
```

```python
import functools

import jax
import jax.numpy as jnp
from jax import lax
from jax.experimental import pallas as pl
from jax.experimental.pallas import tpu as pltpu
from jax.sharding import Mesh
from jax.sharding import PartitionSpec as P

ROUTE_SCALE = 2.5
AXES = ("x", "y", "z", "core")
ORDERS = (("x", "y", "z"), ("y", "z", "x"), ("z", "x", "y"))
PAD = 128
COUNTS = (22, 21, 21)
COLS = 512


def pack_kernel(experts, source, hidden, scores, route, o_ref):
    width = hidden.shape[1]
    gates = ROUTE_SCALE * scores[...] / jnp.sum(scores[...], axis=1, keepdims=True)
    ids = route[...]
    for s in range(experts):
        ids = jnp.where(route[...] == experts + s, source[s], ids)
    lane = lax.broadcasted_iota(jnp.int32, (hidden.shape[0], PAD), 1)
    dense = jnp.zeros(lane.shape, jnp.float32)
    for k in range(ids.shape[1]):
        mine = (lane == ids[:, k : k + 1]) | (lane == ids[:, k : k + 1] + experts)
        dense += jnp.where(mine, gates[:, k : k + 1], 0.0)
    high = dense.astype(jnp.bfloat16).astype(jnp.float32)
    o_ref[:, width:] = jnp.where(lane < experts, high, dense - high).astype(o_ref.dtype)
    o_ref[:, :width] = hidden[...]


def pack(hidden, scores, route, source):
    tokens, width = hidden.shape
    whole = pl.BlockSpec(memory_space=pltpu.VMEM)
    return pl.pallas_call(
        functools.partial(pack_kernel, source.shape[0]),
        in_specs=[pl.BlockSpec(memory_space=pltpu.SMEM), whole, whole, whole],
        out_specs=whole,
        out_shape=jax.ShapeDtypeStruct((tokens, width + PAD), hidden.dtype),
        compiler_params=pltpu.CompilerParams(vmem_limit_bytes=8 * 1024 * 1024),
    )(source, hidden, scores, route)


def ffn_kernel(experts, offsets, counts, ids, *refs):
    n = len(counts)
    pieces, weights, outs = refs[:n], refs[n : n + 6], refs[n + 6 : 2 * n + 6]
    x, gate, up, down, act, o, x_sems, w_sems, o_sems = refs[2 * n + 6 :]
    ga, gb, ua, ub, da, db = weights
    width, hid = ga.shape
    starts = [sum(counts[:j]) for j in range(n)]
    arrive = [
        pltpu.make_async_copy(
            pieces[j].at[pl.ds(offsets[j], counts[j])],
            x.at[pl.ds(starts[j], counts[j])],
            x_sems.at[j],
        )
        for j in range(n)
    ]
    load = [
        pltpu.make_async_copy(ga, gate.at[0], w_sems.at[0]),
        pltpu.make_async_copy(ua, up.at[0], w_sems.at[1]),
        pltpu.make_async_copy(gb, gate.at[1], w_sems.at[2]),
        pltpu.make_async_copy(ub, up.at[1], w_sems.at[3]),
        pltpu.make_async_copy(da, down.at[pl.ds(0, hid)], w_sems.at[4]),
        pltpu.make_async_copy(db, down.at[pl.ds(hid, hid)], w_sems.at[5]),
    ]
    load[0].start()
    for copy in arrive[:2]:
        copy.start()
    load[0].wait()
    gates = []
    for j in range(n):
        arrive[j].wait()
        if j == 0:
            for copy in arrive[2:]:
                copy.start()
            load[1].start()
        rows = x[starts[j] : starts[j] + counts[j], :width]
        gates.append(jnp.dot(rows, gate[0], preferred_element_type=jnp.float32))
    for k in range(2):
        if k == 0:
            g = jnp.concatenate(gates)
        else:
            load[2].wait()
            load[4].start()
            load[5].start()
            g = jnp.dot(x[:, :width], gate[k], preferred_element_type=jnp.float32)
        load[2 * k + 1].wait()
        if k == 0:
            load[2].start()
            load[3].start()
        u = jnp.dot(x[:, :width], up[k], preferred_element_type=jnp.float32)
        shares = x[:, width:].astype(jnp.float32)
        lane = lax.broadcasted_iota(jnp.int32, shares.shape, 1)
        mine = (lane == ids[k]) | (lane == ids[k] + experts)
        share = jnp.sum(jnp.where(mine, shares, 0.0), axis=1, keepdims=True)
        act[:, k * hid : (k + 1) * hid] = (g / (1.0 + jnp.exp(-g)) * u * share).astype(act.dtype)
    load[4].wait()
    load[5].wait()
    leave = []
    for i, c in enumerate(range(0, width, COLS)):
        part = jnp.dot(act[...], down[:, c : c + COLS], preferred_element_type=jnp.float32)
        o[:, c : c + COLS] = part.astype(o.dtype)
        for j in range(n):
            copy = pltpu.make_async_copy(
                o.at[pl.ds(starts[j], counts[j]), pl.ds(c, COLS)],
                outs[j].at[:, pl.ds(c, COLS)],
                o_sems.at[i, j],
            )
            copy.start()
            leave.append(copy)
    for copy in leave:
        copy.wait()


def ffn(ids, pieces, weights, experts, half=None):
    width, hid = weights[0].shape
    offsets, counts = (0,) * len(pieces), tuple(piece.shape[0] for piece in pieces)
    if half is not None:
        cuts = tuple(-(-count // 32) * 16 for count in counts)
        rests = tuple(count - cut for count, cut in zip(counts, cuts))
        offsets, counts = (offsets, cuts) if half == 0 else (cuts, rests)
    amount, n = sum(counts), len(counts)
    anywhere = pl.BlockSpec(memory_space=pl.ANY)
    return pl.pallas_call(
        functools.partial(ffn_kernel, experts, offsets, counts),
        in_specs=[pl.BlockSpec(memory_space=pltpu.SMEM)] + [anywhere] * (n + 6),
        out_specs=[anywhere] * n,
        scratch_shapes=[
            pltpu.VMEM((amount, width + PAD), jnp.bfloat16),
            pltpu.VMEM((2, width, hid), jnp.bfloat16),
            pltpu.VMEM((2, width, hid), jnp.bfloat16),
            pltpu.VMEM((2 * hid, width), jnp.bfloat16),
            pltpu.VMEM((amount, 2 * hid), jnp.bfloat16),
            pltpu.VMEM((amount, width), jnp.bfloat16),
            pltpu.SemaphoreType.DMA((n,)),
            pltpu.SemaphoreType.DMA((6,)),
            pltpu.SemaphoreType.DMA((width // COLS, n)),
        ],
        out_shape=[jax.ShapeDtypeStruct((count, width), jnp.bfloat16) for count in counts],
        compiler_params=pltpu.CompilerParams(vmem_limit_bytes=50 * 1024 * 1024),
        cost_estimate=pl.CostEstimate(
            flops=amount * width * hid * 12,
            bytes_accessed=amount * width * 4 + 12 * width * hid,
            transcendentals=amount * hid * 2,
        ),
    )(ids, *pieces, *weights)


def ring(axis, size, way):
    pairs = []
    for i in range(size):
        pairs += [(2 * i, (i + way) % size * 2), (2 * i + 1, (i - way) % size * 2 + 1)]
    return lambda block: lax.ppermute(block, (axis, "core"), pairs)


def meet(axis, size, first):
    pairs = []
    for i in range(size):
        for core in range(2):
            j = i ^ 1 if (core == 0) == first else size - 1 - i
            pairs.append((2 * i + core, 2 * j + core))
    return lambda block: lax.ppermute(block, (axis, "core"), pairs)


def double(block, axis):
    for first in (True, False):
        block = jnp.concatenate((block, meet(axis, lax.axis_size(axis), first)(block)), axis=0)
    return block


def add(one, other):
    return (one.astype(jnp.float32) + other.astype(jnp.float32)).astype(one.dtype)


def halve(totals, axes):
    for first in (False, True):
        halves = [jnp.split(total, 2) for total in totals]
        arrived = lax.optimization_barrier(
            [meet(a, lax.axis_size(a), first)(sent) for a, (_, sent) in zip(axes, halves)]
        )
        totals = [add(kept, other) for (kept, _), other in zip(halves, arrived)]
    return totals


def per_device(hidden, scores, route, source, gate_proj, up_proj, down_proj):
    spots = lax.axis_size("y") * lax.axis_size("z")
    experts = 2 * spots
    tokens, width = hidden.shape
    swap = [(0, 1), (1, 0)]
    packed = pack(hidden, scores, route, source)
    weights = []
    for own in (gate_proj[0], up_proj[0], down_proj[0]):
        weights += [own, lax.ppermute(own, "core", swap)]
    core = lax.axis_index("core")
    pair = (lax.axis_index("y") * lax.axis_size("z") + lax.axis_index("z")) * 2
    ids = jnp.stack((pair + core, pair + 1 - core)).astype(jnp.int32)

    blocks, start = [], 0
    for count in COUNTS:
        blocks.append(packed[start : start + count])
        start += count
    for phase in range(2):
        blocks = [double(block, order[phase]) for block, order in zip(blocks, ORDERS)]
        if phase == 0:
            blocks, weights = lax.optimization_barrier((blocks, weights))
        else:
            blocks = lax.optimization_barrier(blocks)
    sends = [ring(order[2], lax.axis_size(order[2]), 1) for order in ORDERS]
    steps, done = [blocks], []
    for step in range(lax.axis_size("x") - 1):
        arriving = [send(block) for send, block in zip(sends, steps[-1])]
        done.append(ffn(ids, steps[-1], weights, experts))
        arriving, done[-1] = lax.optimization_barrier((arriving, done[-1]))
        steps.append(arriving)
    backs = [ring(order[2], lax.axis_size(order[2]), -1) for order in ORDERS]
    head = ffn(ids, steps[-1], weights, experts, 0)
    early = [back(t) for back, t in zip(backs, head)]
    tail = ffn(ids, steps[-1], weights, experts, 1)
    early, tail = lax.optimization_barrier((early, tail))
    late = lax.optimization_barrier([back(t) for back, t in zip(backs, tail)])
    arrived = (early, late)
    arrived = [jnp.concatenate(pair, axis=0) for pair in zip(*arrived)]
    for pieces in done[::-1]:
        if arrived is None:
            arrived = lax.optimization_barrier([back(t) for back, t in zip(backs, totals)])
        totals, arrived = [add(*pair) for pair in zip(arrived, pieces)], None
    for phase in (1, 0):
        totals = halve(totals, [order[phase] for order in ORDERS])
    return jnp.concatenate(totals, axis=0)


def solution(mesh):
    planes, experts = mesh.shape["dp"], mesh.shape["expert"]
    side = int(round((experts // 2) ** 0.5))
    grid = Mesh(mesh.devices.reshape(planes, side, side, 2), AXES)
    rows, held = P(AXES, None), ("y", "z", "core")
    placed = (
        rows,
        rows,
        rows,
        P(),
        P(held, None, "x"),
        P(held, None, "x"),
        P(held, "x", None),
    )
    return jax.shard_map(
        per_device, mesh=grid, in_specs=placed, out_specs=rows, check_vma=False
    )
```

```python
import functools

import jax
import jax.numpy as jnp
from jax import lax
from jax.experimental import pallas as pl
from jax.experimental.pallas import tpu as pltpu
from jax.sharding import Mesh
from jax.sharding import PartitionSpec as P

ROUTE_SCALE = 2.5
AXES = ("x", "y", "z", "core")
ORDERS = (("x", "y", "z"), ("y", "z", "x"), ("z", "x", "y"))
PAD = 128
COUNTS = (22, 21, 21)
COLS = 512


def pack_kernel(experts, source, hidden, scores, route, o_ref):
    width = hidden.shape[1]
    gates = ROUTE_SCALE * scores[...] / jnp.sum(scores[...], axis=1, keepdims=True)
    ids = route[...]
    for s in range(experts):
        ids = jnp.where(route[...] == experts + s, source[s], ids)
    lane = lax.broadcasted_iota(jnp.int32, (hidden.shape[0], PAD), 1)
    dense = jnp.zeros(lane.shape, jnp.float32)
    for k in range(ids.shape[1]):
        mine = (lane == ids[:, k : k + 1]) | (lane == ids[:, k : k + 1] + experts)
        dense += jnp.where(mine, gates[:, k : k + 1], 0.0)
    high = dense.astype(jnp.bfloat16).astype(jnp.float32)
    o_ref[:, width:] = jnp.where(lane < experts, high, dense - high).astype(o_ref.dtype)
    o_ref[:, :width] = hidden[...]


def pack(hidden, scores, route, source):
    tokens, width = hidden.shape
    whole = pl.BlockSpec(memory_space=pltpu.VMEM)
    return pl.pallas_call(
        functools.partial(pack_kernel, source.shape[0]),
        in_specs=[pl.BlockSpec(memory_space=pltpu.SMEM), whole, whole, whole],
        out_specs=whole,
        out_shape=jax.ShapeDtypeStruct((tokens, width + PAD), hidden.dtype),
        compiler_params=pltpu.CompilerParams(vmem_limit_bytes=8 * 1024 * 1024),
    )(source, hidden, scores, route)


def ffn_kernel(experts, offsets, counts, ids, *refs):
    n = len(counts)
    pieces, weights, outs = refs[:n], refs[n : n + 6], refs[n + 6 : 2 * n + 6]
    x, gate, up, down, act, o, x_sems, w_sems, o_sems = refs[2 * n + 6 :]
    ga, gb, ua, ub, da, db = weights
    width, hid = ga.shape
    starts = [sum(counts[:j]) for j in range(n)]
    arrive = [
        pltpu.make_async_copy(
            pieces[j].at[pl.ds(offsets[j], counts[j])],
            x.at[pl.ds(starts[j], counts[j])],
            x_sems.at[j],
        )
        for j in range(n)
    ]
    load = [
        pltpu.make_async_copy(ga, gate.at[0], w_sems.at[0]),
        pltpu.make_async_copy(ua, up.at[0], w_sems.at[1]),
        pltpu.make_async_copy(gb, gate.at[1], w_sems.at[2]),
        pltpu.make_async_copy(ub, up.at[1], w_sems.at[3]),
        pltpu.make_async_copy(da, down.at[pl.ds(0, hid)], w_sems.at[4]),
        pltpu.make_async_copy(db, down.at[pl.ds(hid, hid)], w_sems.at[5]),
    ]
    load[0].start()
    for copy in arrive[:2]:
        copy.start()
    load[0].wait()
    gates = []
    for j in range(n):
        arrive[j].wait()
        if j == 0:
            for copy in arrive[2:]:
                copy.start()
            load[1].start()
        rows = x[starts[j] : starts[j] + counts[j], :width]
        gates.append(jnp.dot(rows, gate[0], preferred_element_type=jnp.float32))
    for k in range(2):
        if k == 0:
            g = jnp.concatenate(gates)
        else:
            load[2].wait()
            load[4].start()
            load[5].start()
            g = jnp.dot(x[:, :width], gate[k], preferred_element_type=jnp.float32)
        load[2 * k + 1].wait()
        if k == 0:
            load[2].start()
            load[3].start()
        u = jnp.dot(x[:, :width], up[k], preferred_element_type=jnp.float32)
        shares = x[:, width:].astype(jnp.float32)
        lane = lax.broadcasted_iota(jnp.int32, shares.shape, 1)
        mine = (lane == ids[k]) | (lane == ids[k] + experts)
        share = jnp.sum(jnp.where(mine, shares, 0.0), axis=1, keepdims=True)
        act[:, k * hid : (k + 1) * hid] = (g / (1.0 + jnp.exp(-g)) * u * share).astype(act.dtype)
    load[4].wait()
    load[5].wait()
    leave = []
    for i, c in enumerate(range(0, width, COLS)):
        part = jnp.dot(act[...], down[:, c : c + COLS], preferred_element_type=jnp.float32)
        o[:, c : c + COLS] = part.astype(o.dtype)
        for j in range(n):
            copy = pltpu.make_async_copy(
                o.at[pl.ds(starts[j], counts[j]), pl.ds(c, COLS)],
                outs[j].at[:, pl.ds(c, COLS)],
                o_sems.at[i, j],
            )
            copy.start()
            leave.append(copy)
    for copy in leave:
        copy.wait()


def ffn(ids, pieces, weights, experts, half=None):
    width, hid = weights[0].shape
    offsets, counts = (0,) * len(pieces), tuple(piece.shape[0] for piece in pieces)
    if half is not None:
        cuts = tuple(-(-count // 32) * 16 for count in counts)
        rests = tuple(count - cut for count, cut in zip(counts, cuts))
        offsets, counts = (offsets, cuts) if half == 0 else (cuts, rests)
    amount, n = sum(counts), len(counts)
    anywhere = pl.BlockSpec(memory_space=pl.ANY)
    return pl.pallas_call(
        functools.partial(ffn_kernel, experts, offsets, counts),
        in_specs=[pl.BlockSpec(memory_space=pltpu.SMEM)] + [anywhere] * (n + 6),
        out_specs=[anywhere] * n,
        scratch_shapes=[
            pltpu.VMEM((amount, width + PAD), jnp.bfloat16),
            pltpu.VMEM((2, width, hid), jnp.bfloat16),
            pltpu.VMEM((2, width, hid), jnp.bfloat16),
            pltpu.VMEM((2 * hid, width), jnp.bfloat16),
            pltpu.VMEM((amount, 2 * hid), jnp.bfloat16),
            pltpu.VMEM((amount, width), jnp.bfloat16),
            pltpu.SemaphoreType.DMA((n,)),
            pltpu.SemaphoreType.DMA((6,)),
            pltpu.SemaphoreType.DMA((width // COLS, n)),
        ],
        out_shape=[jax.ShapeDtypeStruct((count, width), jnp.bfloat16) for count in counts],
        compiler_params=pltpu.CompilerParams(vmem_limit_bytes=50 * 1024 * 1024),
        cost_estimate=pl.CostEstimate(
            flops=amount * width * hid * 12,
            bytes_accessed=amount * width * 4 + 12 * width * hid,
            transcendentals=amount * hid * 2,
        ),
    )(ids, *pieces, *weights)


def ring(axis, size, way):
    pairs = []
    for i in range(size):
        pairs += [(2 * i, (i + way) % size * 2), (2 * i + 1, (i - way) % size * 2 + 1)]
    return lambda block: lax.ppermute(block, (axis, "core"), pairs)


def meet(axis, size, first):
    pairs = []
    for i in range(size):
        for core in range(2):
            j = i ^ 1 if (core == 0) == first else size - 1 - i
            pairs.append((2 * i + core, 2 * j + core))
    return lambda block: lax.ppermute(block, (axis, "core"), pairs)


def double(block, axis):
    for first in (True, False):
        block = jnp.concatenate((block, meet(axis, lax.axis_size(axis), first)(block)), axis=0)
    return block


def add(one, other):
    return (one.astype(jnp.float32) + other.astype(jnp.float32)).astype(one.dtype)


def halve(totals, axes, hold):
    for first in (False, True):
        halves = [jnp.split(total, 2) for total in totals]
        arrived = [meet(a, lax.axis_size(a), first)(sent) for a, (_, sent) in zip(axes, halves)]
        if hold:
            arrived = lax.optimization_barrier(arrived)
        totals = [add(kept, other) for (kept, _), other in zip(halves, arrived)]
    return totals


def per_device(hidden, scores, route, source, gate_proj, up_proj, down_proj):
    spots = lax.axis_size("y") * lax.axis_size("z")
    experts = 2 * spots
    tokens, width = hidden.shape
    swap = [(0, 1), (1, 0)]
    packed = pack(hidden, scores, route, source)
    weights = []
    for own in (gate_proj[0], up_proj[0], down_proj[0]):
        weights += [own, lax.ppermute(own, "core", swap)]
    core = lax.axis_index("core")
    pair = (lax.axis_index("y") * lax.axis_size("z") + lax.axis_index("z")) * 2
    ids = jnp.stack((pair + core, pair + 1 - core)).astype(jnp.int32)

    blocks, start = [], 0
    for count in COUNTS:
        blocks.append(packed[start : start + count])
        start += count
    for phase in range(2):
        blocks = [double(block, order[phase]) for block, order in zip(blocks, ORDERS)]
        if phase == 0:
            blocks, weights = lax.optimization_barrier((blocks, weights))
        else:
            blocks = lax.optimization_barrier(blocks)
    sends = [ring(order[2], lax.axis_size(order[2]), 1) for order in ORDERS]
    steps, done = [blocks], []
    for step in range(lax.axis_size("x") - 1):
        arriving = [send(block) for send, block in zip(sends, steps[-1])]
        done.append(ffn(ids, steps[-1], weights, experts))
        arriving, done[-1] = lax.optimization_barrier((arriving, done[-1]))
        steps.append(arriving)
    backs = [ring(order[2], lax.axis_size(order[2]), -1) for order in ORDERS]
    head = ffn(ids, steps[-1], weights, experts, 0)
    early = [back(t) for back, t in zip(backs, head)]
    tail = ffn(ids, steps[-1], weights, experts, 1)
    early, tail = lax.optimization_barrier((early, tail))
    late = lax.optimization_barrier([back(t) for back, t in zip(backs, tail)])
    arrived = (early, late)
    arrived = [jnp.concatenate(pair, axis=0) for pair in zip(*arrived)]
    for pieces in done[::-1]:
        if arrived is None:
            arrived = lax.optimization_barrier([back(t) for back, t in zip(backs, totals)])
        totals, arrived = [add(*pair) for pair in zip(arrived, pieces)], None
    for phase in (1, 0):
        totals = halve(totals, [order[phase] for order in ORDERS], phase == 1)
    return jnp.concatenate(totals, axis=0)


def solution(mesh):
    planes, experts = mesh.shape["dp"], mesh.shape["expert"]
    side = int(round((experts // 2) ** 0.5))
    grid = Mesh(mesh.devices.reshape(planes, side, side, 2), AXES)
    rows, held = P(AXES, None), ("y", "z", "core")
    placed = (
        rows,
        rows,
        rows,
        P(),
        P(held, None, "x"),
        P(held, None, "x"),
        P(held, "x", None),
    )
    return jax.shard_map(
        per_device, mesh=grid, in_specs=placed, out_specs=rows, check_vma=False
    )
```
